128 devices in a mesh: row: 8 (over z_lo, y), col: 16 (over z_hi, x, core).
Axes of the slice: x: 4, y: 4, z: 4 (z_hi: 2, z_lo: 2; z = z_hi * 2 + z_lo), core: 2. Of those that a mesh axis runs over, the one named last changes fastest.
Arguments:
- object_field: float32 [2, 2048, 4096], P(None, 'row', 'col'), may hold values from -6 to 6
- probe_modes: float32 [4, 2, 256, 256], replicated, may hold values from -3 to 3
- positions: int32 [8, 16, 6, 2], P('row', 'col'), may hold values from 0 to 255
- counts: int32 [8, 16], P('row', 'col'), may hold values from 0 to 6, as said below
- amplitude: float32 [8, 16, 6, 256, 256], P('row', 'col'), may hold values from 0 to 2
Outputs:
- updated: float32 [2, 2048, 4096], P(None, 'row', 'col')
The draws below stay inside these ranges and needn't reach their ends.
Inputs may be any that keep to these rules, and one draw needn't show every extreme that they name: The counts of two tiles in one tile row whose column indices differ by 8 add up to 6; some tile has exactly 6. Only positions below a tile's count are used.
All inputs are finite; a program needn't handle non-finite values.
Results may differ from the reference program's by a relative error of at most 0.0018.
Values sent between devices are 32-bit elements; how exact they have to be, the bound alone decides.
No kernel may reach another device: no remote copies, remote signals or barrier semaphores. Data moves between devices by JAX's collectives and lax.ppermute only.
A program may use at most 64 MiB of HBM per device.

```python
import math
import jax
import jax.numpy as jnp
from jax import lax

PATCH = 256
MODES = 4
TILE = 256
SLOTS = 3
ITERS = 2
SURPLUS = 3
MOST = 6
TILES_R = 8
TILES_C = 16
ROWS = 2048
COLS = 4096


def draw_counts(key, part):
    half = TILES_C // 2
    first = jax.random.fold_in(key, 11)
    second = jax.random.fold_in(key, 23)
    base = jax.random.randint(first, (TILES_R, half), SLOTS - SURPLUS, SLOTS + SURPLUS + 1)
    spot = jax.random.randint(second, (), 0, TILES_R * half)
    flat = jnp.where(jnp.arange(TILES_R * half) == spot, MOST, base.reshape(-1))
    base = flat.reshape(TILES_R, half)
    return jnp.concatenate([base, 2 * SLOTS - base], axis=1).astype(jnp.int32)


def set_ends(result, own_key, least, top_value):
    longest = result.shape.index(max(result.shape))
    spots = []
    for shift in (0, 1):
        where = [jax.random.randint(jax.random.fold_in(own_key, axis), (), 0, length) for axis, length in enumerate(result.shape)]
        where[longest] = (where[longest] + shift) % result.shape[longest]
        spots.append(tuple(where))
    return result.at[spots[0]].set(least).at[spots[1]].set(top_value)


def shard_levels(key, dims, split, least, largest):
    def one(dim, shards_of):
        heights = jax.random.uniform(jax.random.fold_in(jax.random.fold_in(key, 6), dim), (shards_of,), jnp.float32, least / len(split), largest / len(split))
        return jnp.repeat(jnp.exp(heights), dims[dim] // shards_of).reshape((-1,) + (1,) * (len(dims) - dim - 1))

    gain = one(*split[0])
    for cut in split[1:]:
        gain = gain * one(*cut)
    return gain


def scatter_about(key, extent, deviation, most, shards=(), held_as=jnp.bfloat16):
    entries = jax.random.normal(key, extent, jnp.float32) * deviation
    if len(shards) > 0:
        entries = shard_levels(key, extent, shards, -0.22, 0.18) * entries
    return jnp.clip(entries, min=-most, max=most).astype(held_as)


def setup_inputs(seed: int = 0) -> dict:
    splits = jax.random.split(jax.random.key(seed), 6)
    return {
        "object_field": scatter_about(splits[0], (2, ROWS, COLS), 1.0, 6.0, ((1, 8), (2, 16)), jnp.float32),
        "probe_modes": scatter_about(splits[1], (MODES, 2, PATCH, PATCH), 0.5, 3.0, (), jnp.float32),
        "positions": set_ends(jax.random.randint(splits[2], (TILES_R, TILES_C, MOST, 2), 0, TILE), jax.random.fold_in(splits[2], 1), 0, TILE - 1).astype(jnp.int32),
        "counts": draw_counts(jax.random.fold_in(splits[5], 71), 0),
        "amplitude": jnp.clip(2.0 * jax.random.uniform(splits[4], (TILES_R, TILES_C, MOST, PATCH, PATCH), jnp.float32) ** shard_levels(splits[4], (TILES_R, TILES_C, MOST, PATCH, PATCH), ((0, 8), (1, 16)), -0.2, 0.2), 0.0, 2.0),
    }


step_size = 0.1
damping = 0.1

def blocks(upper_left, upper_right, lower_left, lower_right):
    return jnp.stack([jnp.stack([upper_left, upper_right], axis=1), jnp.stack([lower_left, lower_right], axis=1)], axis=0)

def tables():
    ladder = jnp.arange(PATCH, dtype=jnp.int32)
    product = ladder[:, None] * ladder[None, :] % PATCH
    theta = product.astype(jnp.float32) * (2.0 * math.pi / PATCH)
    factor = 1.0 / math.sqrt(PATCH)
    cosine = jnp.cos(theta) * factor
    minus_sine = -jnp.sin(theta) * factor
    table_fwd = blocks(cosine, -minus_sine, minus_sine, cosine).astype(jnp.bfloat16)
    table_inv = blocks(cosine, minus_sine, -minus_sine, cosine).astype(jnp.bfloat16)
    return (table_fwd, table_inv)

def left_mult(table, values):
    return jnp.einsum('cjdk,mdkl->mcjl', table.astype(jnp.float32), values.astype(jnp.float32), precision=lax.Precision.HIGHEST)

def right_mult(values, table):
    return jnp.einsum('mcjk,ckdl->mdjl', values.astype(jnp.float32), table.astype(jnp.float32), precision=lax.Precision.HIGHEST)

def patch_gradient(patch, measured, probe_modes, table_fwd, table_inv):
    probe_re = probe_modes[:, 0]
    probe_im = probe_modes[:, 1]
    psi = jnp.stack([probe_re * patch[0] - probe_im * patch[1], probe_re * patch[1] + probe_im * patch[0]], axis=1).astype(jnp.bfloat16)
    section = left_mult(table_fwd, psi).astype(jnp.bfloat16)
    far = right_mult(section, table_inv)
    intensity = lax.optimization_barrier(jnp.sum(far * far, axis=(0, 1)))
    ratio = 1.0 - measured / jnp.sqrt(intensity + damping)
    chi = (far * ratio).astype(jnp.bfloat16)
    back = left_mult(table_inv, chi).astype(jnp.bfloat16)
    wave = right_mult(back, table_fwd)
    grad_re = lax.optimization_barrier(jnp.sum(probe_re * wave[:, 0] + probe_im * wave[:, 1], axis=0))
    grad_im = lax.optimization_barrier(jnp.sum(probe_re * wave[:, 1] - probe_im * wave[:, 0], axis=0))
    return jnp.stack([grad_re, grad_im], axis=0)

def reference(object_field, probe_modes, positions, counts, amplitude):
    table_fwd, table_inv = tables()
    tile_rows, tile_cols = counts.shape
    slot_ids = jnp.arange(MOST, dtype=jnp.int32)
    live = (slot_ids[None, None, :] < counts[:, :, None]).reshape(-1)
    order = jnp.argsort(jnp.where(live, 0, 1).astype(jnp.int32), stable=True)[:SLOTS * tile_rows * tile_cols].astype(jnp.int32)
    tile_row = order // (tile_cols * MOST)
    tile_col = order // MOST % tile_cols
    offsets = positions.reshape(-1, 2)
    top_rows = (tile_row * TILE + offsets[order, 0]).astype(jnp.int32)
    left_cols = (tile_col * TILE + offsets[order, 1]).astype(jnp.int32)
    measured_all = amplitude.reshape(-1, PATCH, PATCH)
    anchor = jnp.int32(0)
    field = object_field
    for sweep in range(ITERS):
        padded = jnp.pad(field, ((0, 0), (0, PATCH), (0, PATCH)))

        def visit(total, entry):
            which, top, left = entry
            patch = lax.dynamic_slice(padded, (anchor, top, left), (2, PATCH, PATCH))
            measured = lax.dynamic_index_in_dim(measured_all, which, 0, keepdims=False)
            grads = patch_gradient(patch, measured, probe_modes, table_fwd, table_inv)
            current = lax.dynamic_slice(total, (anchor, top, left), (2, PATCH, PATCH))
            return (lax.dynamic_update_slice(total, current + grads, (anchor, top, left)), None)
        total, unused = lax.scan(visit, jnp.zeros_like(padded), (order, top_rows, left_cols))
        field = field - step_size * total[:, :ROWS, :COLS]
    return field
```

```python
import math

import jax
import jax.numpy as jnp
import ml_dtypes
import numpy as np
from jax import lax
from jax.experimental import pallas as pl
from jax.experimental.pallas import tpu as pltpu
from jax.sharding import PartitionSpec as P

ITERS = 2
STEP = 0.1
DAMPING = 0.1
SIDE = 256
HALF = 128
F32 = jnp.float32
BF16 = jnp.bfloat16
VMEM = pl.BlockSpec(memory_space=pltpu.VMEM)
SMEM = pl.BlockSpec(memory_space=pltpu.SMEM)


def from_behind(block, axis, distance):
    devices = range(lax.axis_size(axis))
    route = [(i - distance, i) for i in devices if i - distance in devices]
    return lax.ppermute(block, axis, route)


def tables():
    ladder = np.arange(SIDE, dtype=np.int32)
    theta = (ladder[:, None] * ladder[None, :] % SIDE).astype(np.float32)
    theta = theta * np.float32(2.0 * math.pi / SIDE)
    factor = np.float32(1.0 / math.sqrt(SIDE))
    cosine, sine = np.cos(theta) * factor, np.sin(theta) * factor
    forms = []
    for parity in (0, 1):
        c, s = cosine[parity::2, :HALF], sine[parity::2, :HALF]
        forms.append(np.block([[c, s], [-s, c]]))
    forms += [f.T for f in forms]
    return np.stack(forms).astype(ml_dtypes.bfloat16)


def parity_order():
    order = np.concatenate([np.arange(0, SIDE, 2), np.arange(1, SIDE, 2)])
    matrix = np.zeros((SIDE, SIDE), np.float32)
    matrix[order, np.arange(SIDE)] = 1.0
    return matrix


def sort_kernel(order_ref, flip_ref, amp_ref, out_ref):
    exact = dict(preferred_element_type=F32, precision=lax.Precision.HIGHEST)
    wide = jnp.dot(amp_ref[0], order_ref[...], **exact)
    out_ref[0] = jnp.dot(flip_ref[...], wide, **exact)


def sort_amplitude(amplitude):
    most = amplitude.shape[0]
    order = parity_order()
    whole = pl.BlockSpec((SIDE, SIDE), lambda s: (0, 0))
    one = pl.BlockSpec((1, SIDE, SIDE), lambda s: (s, 0, 0))
    return pl.pallas_call(
        sort_kernel,
        grid=(most,),
        out_shape=jax.ShapeDtypeStruct(amplitude.shape, F32),
        in_specs=[whole, whole, one],
        out_specs=one,
        cost_estimate=pl.CostEstimate(
            flops=most * 24 * SIDE**3, bytes_accessed=8 * amplitude.size, transcendentals=0
        ),
    )(order, np.ascontiguousarray(order.T), amplitude)


def dot(a, b):
    return jnp.dot(a, b, preferred_element_type=F32)


def lanes(a, b):
    return jnp.concatenate([a, b], axis=1)


def rows(a, b):
    return jnp.concatenate([a, b], axis=0)


def update_kernel(
    offsets_ref,
    count_ref,
    own_ref,
    below_ref,
    right_ref,
    diag_ref,
    probe_ref,
    amp_ref,
    table_ref,
    own_out,
    below_out,
    right_out,
    diag_out,
    patch,
    far,
    level,
    grad,
):
    modes = probe_ref.shape[0]
    outs = (own_out, below_out, right_out, diag_out)
    for out in outs:
        out[...] = jnp.zeros_like(out)
    row = lax.broadcasted_iota(jnp.int32, (SIDE, SIDE), 0)
    column = lax.broadcasted_iota(jnp.int32, (SIDE, SIDE), 1)

    def position(slot, _):
        top, left = offsets_ref[slot, 0], offsets_ref[slot, 1]
        here, beside = row >= top, column >= left
        for part in (0, 1):
            mixed = jnp.where(
                here,
                jnp.where(beside, own_ref[part], right_ref[part]),
                jnp.where(beside, below_ref[part], diag_ref[part]),
            )
            mixed = pltpu.roll(mixed, lax.rem(SIDE - left, SIDE), 1)
            patch[part] = pltpu.roll(mixed, lax.rem(SIDE - top, SIDE), 0)
        for m in range(modes):
            sums, differences = [], []
            psi = []
            for half in (0, 1):
                at = pl.ds(half * HALF, HALF)
                pr, pi = probe_ref[m, 0, at, :], probe_ref[m, 1, at, :]
                xr, xi = patch[0, at, :], patch[1, at, :]
                psi.append(rows(pr * xr - pi * xi, pr * xi + pi * xr))
            even = dot(table_ref[0], (psi[0] + psi[1]).astype(BF16))
            odd = dot(table_ref[1], (psi[0] - psi[1]).astype(BF16))
            for s in (even, odd):
                a, b = s[:, :HALF], s[:, HALF:]
                u, v = (a + b).astype(BF16), (a - b).astype(BF16)
                sums.append(lanes(u[:HALF], u[HALF:]))
                differences.append(lanes(v[:HALF], v[HALF:]))
            for q, block in ((0, rows(*sums)), (1, rows(*differences))):
                f = dot(block, table_ref[2 + q])
                far[m, q] = f
                power = f[:, :HALF] * f[:, :HALF] + f[:, HALF:] * f[:, HALF:]
                at = pl.ds(q * HALF, HALF)
                if m:
                    power = power + level[:, at]
                level[:, at] = power
        level[...] = 1.0 - amp_ref[slot] / jnp.sqrt(level[...] + DAMPING)
        for m in range(modes):
            chi = []
            for q in (0, 1):
                ratio = level[:, q * HALF : (q + 1) * HALF]
                chi.append((far[m, q] * lanes(ratio, ratio)).astype(BF16))
            halves = []
            for parity in (0, 1):
                c = [x[parity * HALF : (parity + 1) * HALF] for x in chi]
                real = lanes(c[0][:, :HALF], c[1][:, :HALF])
                imag = lanes(c[0][:, HALF:], c[1][:, HALF:])
                halves.append(dot(table_ref[2 + parity], rows(real, imag)))
            top_back = (halves[0] + halves[1]).astype(BF16)
            bottom_back = (halves[0] - halves[1]).astype(BF16)
            wave = []
            for q in (0, 1):
                at = slice(q * HALF, (q + 1) * HALF)
                block = rows(
                    lanes(top_back[:HALF, at], top_back[HALF:, at]),
                    lanes(bottom_back[:HALF, at], bottom_back[HALF:, at]),
                )
                wave.append(dot(block, table_ref[q]))
            for side, w in ((0, wave[0] + wave[1]), (1, wave[0] - wave[1])):
                at = pl.ds(side * HALF, HALF)
                pr, pi = probe_ref[m, 0, :, at], probe_ref[m, 1, :, at]
                wr, wi = w[:, :HALF], w[:, HALF:]
                gr, gi = pr * wr + pi * wi, pr * wi - pi * wr
                if m:
                    gr, gi = gr + grad[0, :, at], gi + grad[1, :, at]
                grad[0, :, at] = gr
                grad[1, :, at] = gi
        for part in (0, 1):
            turned = pltpu.roll(pltpu.roll(grad[part], top, 0), left, 1)
            upper, lower = jnp.where(here, turned, 0.0), jnp.where(here, 0.0, turned)
            own_out[part] += jnp.where(beside, upper, 0.0)
            right_out[part] += jnp.where(beside, 0.0, upper)
            below_out[part] += jnp.where(beside, lower, 0.0)
            diag_out[part] += jnp.where(beside, 0.0, lower)
        return 0

    lax.fori_loop(0, count_ref[0], position, 0)


def gradient(offsets, count, own, below, right, diag, probe, amplitude, table):
    modes = probe.shape[0]
    tile = (2, SIDE, SIDE)
    return pl.pallas_call(
        update_kernel,
        out_shape=[jax.ShapeDtypeStruct(tile, F32)] * 4,
        in_specs=[SMEM, SMEM] + [VMEM] * 7,
        out_specs=[VMEM] * 4,
        scratch_shapes=[
            pltpu.VMEM(tile, F32),
            pltpu.VMEM((modes, 2, SIDE, SIDE), F32),
            pltpu.VMEM((SIDE, SIDE), F32),
            pltpu.VMEM(tile, F32),
        ],
        compiler_params=pltpu.CompilerParams(vmem_limit_bytes=48 * 2**20),
    )(offsets, count, own, below, right, diag, probe, amplitude, table)


def body(object_field, probe_modes, positions, counts, amplitude):
    table = tables()
    count = counts[0]
    offsets = positions[0, 0]
    sorted_amp = sort_amplitude(amplitude[0, 0])
    field = object_field
    for sweep in range(ITERS):
        below = from_behind(field, "row", -1)
        right = from_behind(field, "col", -1)
        diag = from_behind(below, "col", -1)
        own_sum, below_sum, right_sum, diag_sum = gradient(
            offsets, count, field, below, right, diag, probe_modes, sorted_amp, table
        )
        below_sum = below_sum + from_behind(diag_sum, "col", 1)
        total = own_sum + from_behind(right_sum, "col", 1) + from_behind(below_sum, "row", 1)
        field = field - STEP * total
    return field


def solution(mesh):
    placed = (
        P(None, "row", "col"),
        P(),
        P("row", "col", None, None),
        P("row", "col"),
        P("row", "col", None, None, None),
    )
    return jax.shard_map(
        body, mesh=mesh, in_specs=placed, out_specs=P(None, "row", "col"), check_vma=False
    )
```

```python
import functools
import math

import jax
import jax.numpy as jnp
import ml_dtypes
import numpy as np
from jax import lax
from jax.experimental import pallas as pl
from jax.experimental.pallas import tpu as pltpu
from jax.sharding import PartitionSpec as P

ITERS = 2
STEP = 0.1
DAMPING = 0.1
SIDE = 256
HALF = 128
SUB = 8
CHUNK = 16
H_SPLIT = [[False, False, True, True], [True, False, True, True]]
G_SPLIT = [[True, False, True, True], [True, False, True, True]]
AHEAD = 1
F32 = jnp.float32
BF16 = jnp.bfloat16
VMEM = pl.BlockSpec(memory_space=pltpu.VMEM)
SMEM = pl.BlockSpec(memory_space=pltpu.SMEM)


def from_behind(block, axis, distance):
    devices = range(lax.axis_size(axis))
    route = [(i - distance, i) for i in devices if i - distance in devices]
    return lax.ppermute(block, axis, route)


def tables():
    ladder = np.arange(SIDE, dtype=np.int32)
    theta = (ladder[:, None] * ladder[None, :] % SIDE).astype(np.float32)
    theta = theta * np.float32(2.0 * math.pi / SIDE)
    factor = np.float32(1.0 / math.sqrt(SIDE))
    cosine, sine = np.cos(theta) * factor, np.sin(theta) * factor
    forms = []
    for parity in (0, 1):
        c, s = cosine[parity::2, :HALF], sine[parity::2, :HALF]
        forms.append(np.block([[c, s], [-s, c]]))
    forms += [f.T for f in forms]
    return np.stack(forms).astype(ml_dtypes.bfloat16)


def parity_order():
    order = np.concatenate([np.arange(0, SIDE, 2), np.arange(1, SIDE, 2)])
    matrix = np.zeros((SIDE, SIDE), np.float32)
    matrix[order, np.arange(SIDE)] = 1.0
    return matrix.astype(ml_dtypes.bfloat16)


def sort_kernel(order_ref, amp_ref, out_ref, wide):
    def one(slot, _):
        rest, terms = amp_ref[slot], []
        for _ in range(3):
            terms.append(rest.astype(BF16))
            rest = rest - terms[-1].astype(F32)
        moved = [dot(term, order_ref[...]) for term in terms]
        whole = (moved[0] + moved[1]) + moved[2]
        for q in (0, 1):
            at = slice(q * HALF, (q + 1) * HALF)
            wide[q] = whole[:, at]
            for parity in (0, 1):
                rows_at = pl.ds(parity * HALF, HALF)
                out_ref[slot, rows_at, at] = wide[q, pl.ds(parity, HALF, stride=2), :]
        return 0

    lax.fori_loop(0, amp_ref.shape[0], one, 0)


def sort_amplitude(amplitude):
    return pl.pallas_call(
        sort_kernel,
        out_shape=jax.ShapeDtypeStruct(amplitude.shape, F32),
        in_specs=[VMEM, VMEM],
        out_specs=VMEM,
        scratch_shapes=[pltpu.VMEM((2, SIDE, HALF), F32)],
        compiler_params=pltpu.CompilerParams(vmem_limit_bytes=16 * 2**20),
        cost_estimate=pl.CostEstimate(
            flops=6 * amplitude.size * SIDE, bytes_accessed=8 * amplitude.size, transcendentals=0
        ),
    )(parity_order(), amplitude)


def dot(a, b):
    return jnp.dot(a, b, preferred_element_type=F32)


def lanes(a, b):
    return jnp.concatenate([a, b], axis=1)


def rows(a, b):
    return jnp.concatenate([a, b], axis=0)


def in_turn(modes, first, second):
    held = []
    for m in range(modes + AHEAD):
        if m < modes:
            held.append(first(m))
        if m >= AHEAD:
            second(m - AHEAD, held[m - AHEAD])


def places(splits):
    found = []
    for index, split in enumerate(splits):
        at = pl.ds(index // 2 * SIDE, SIDE)
        for part in (0, 1) if split else (slice(None),):
            found.append((index % 2, part, at))
    return found


def update_kernel(in_splits, out_splits, offsets_ref, count_ref, *refs):
    tile_at, out_at = places(in_splits), places(out_splits)
    tiles, refs = refs[: len(tile_at)], refs[len(tile_at) :]
    (probe_ref, amp_ref, table_ref), refs = refs[:3], refs[3:]
    outs, scratch = refs[: len(out_at)], refs[len(out_at) :]
    left_ext, right_ext, left_sum, right_sum, patch, far, chis, grad = scratch
    modes = probe_ref.shape[0]
    for tile, (half, part, at) in zip(tiles, tile_at):
        (left_ext, right_ext)[half][part, at] = tile[...]
    left_sum[...] = jnp.zeros_like(left_sum)
    right_sum[...] = jnp.zeros_like(right_sum)
    groups = SIDE // SUB
    column = lax.broadcasted_iota(jnp.int32, (SIDE + SUB, SIDE), 1)
    lane = lax.broadcasted_iota(jnp.int32, (groups, SUB, SIDE), 1)

    def position(slot, _):
        top, left = offsets_ref[0, 0, slot, 0], offsets_ref[0, 0, slot, 1]
        shift = lax.rem(top, SUB)
        window = pl.ds(pl.multiple_of(top - shift, SUB), SIDE + SUB)
        beside = column >= left
        for part in (0, 1):
            mixed = jnp.where(beside, left_ext[part, window, :], right_ext[part, window, :])
            mixed = pltpu.roll(mixed, lax.rem(SIDE - left, SIDE), 1)
            mixed = mixed.reshape(groups + 1, SUB, SIDE)
            mixed = pltpu.roll(mixed, lax.rem(SUB - shift, SUB), 1)
            mixed = jnp.where(lane < SUB - shift, mixed[:-1], mixed[1:])
            patch[part] = mixed.reshape(SIDE, SIDE)
        def section(m):
            psi = []
            for half in (0, 1):
                at = pl.ds(half * HALF, HALF)
                pr, pi = probe_ref[m, 0, at, :], probe_ref[m, 1, at, :]
                xr, xi = patch[0, at, :], patch[1, at, :]
                psi.append(rows(pr * xr - pi * xi, pr * xi + pi * xr))
            even = dot(table_ref[0], (psi[0] + psi[1]).astype(BF16))
            odd = dot(table_ref[1], (psi[0] - psi[1]).astype(BF16))
            sums, differences = [], []
            for s in (even, odd):
                a, b = s[:, :HALF], s[:, HALF:]
                u, v = (a + b).astype(BF16), (a - b).astype(BF16)
                sums.append(lanes(u[:HALF], u[HALF:]))
                differences.append(lanes(v[:HALF], v[HALF:]))
            return rows(*sums), rows(*differences)

        def spread(m, blocks):
            for q, block in enumerate(blocks):
                far[m, q] = dot(block, table_ref[2 + q])

        def back(m):
            halves = []
            for parity in (0, 1):
                at = pl.ds(parity * HALF, HALF)
                c = [chis[m, q, at, :] for q in (0, 1)]
                real = lanes(c[0][:, :HALF], c[1][:, :HALF])
                imag = lanes(c[0][:, HALF:], c[1][:, HALF:])
                halves.append(dot(table_ref[2 + parity], rows(real, imag)))
            top_back = (halves[0] + halves[1]).astype(BF16)
            bottom_back = (halves[0] - halves[1]).astype(BF16)
            blocks = []
            for q in (0, 1):
                at = slice(q * HALF, (q + 1) * HALF)
                blocks.append(
                    rows(
                        lanes(top_back[:HALF, at], top_back[HALF:, at]),
                        lanes(bottom_back[:HALF, at], bottom_back[HALF:, at]),
                    )
                )
            return blocks

        def gather(m, blocks):
            wave = [dot(block, table_ref[q]) for q, block in enumerate(blocks)]
            for side, w in ((0, wave[0] + wave[1]), (1, wave[0] - wave[1])):
                at = pl.ds(side * HALF, HALF)
                pr, pi = probe_ref[m, 0, :, at], probe_ref[m, 1, :, at]
                wr, wi = w[:, :HALF], w[:, HALF:]
                gr, gi = pr * wr + pi * wi, pr * wi - pi * wr
                if m:
                    gr, gi = gr + grad[0, :, at], gi + grad[1, :, at]
                grad[0, :, at] = gr
                grad[1, :, at] = gi

        in_turn(modes, section, spread)
        for q in (0, 1):
            for start in range(0, SIDE, CHUNK):
                at = pl.ds(start, CHUNK)
                f = [far[m, q, at, :] for m in range(modes)]
                squares = [x * x for x in f]
                power = sum(squares[1:], squares[0])
                power = power[:, :HALF] + power[:, HALF:]
                measured = amp_ref[slot, at, q * HALF : (q + 1) * HALF]
                ratio = 1.0 - measured * lax.rsqrt(power + DAMPING)
                ratio = lanes(ratio, ratio)
                for m in range(modes):
                    chis[m, q, at, :] = (f[m] * ratio).astype(BF16)
        in_turn(modes, back, gather)
        empty = jnp.zeros((1, SUB, SIDE), F32)
        for part in (0, 1):
            turned = pltpu.roll(grad[part], left, 1).reshape(groups, SUB, SIDE)
            turned = pltpu.roll(turned, shift, 1)
            first = jnp.concatenate([jnp.where(lane < shift, 0.0, turned), empty], axis=0)
            second = jnp.concatenate([empty, jnp.where(lane < shift, turned, 0.0)], axis=0)
            turned = (first + second).reshape(SIDE + SUB, SIDE)
            left_sum[part, window, :] += jnp.where(beside, turned, 0.0)
            right_sum[part, window, :] += jnp.where(beside, 0.0, turned)
        return 0

    lax.fori_loop(0, count_ref[0, 0], position, 0)
    for out, (half, part, at) in zip(outs, out_at):
        out[...] = (left_sum, right_sum)[half][part, at]


def gradient(offsets, count, own, right, below, diag, probe, amplitude, table, out_splits):
    modes = probe.shape[0]
    tall = pltpu.VMEM((2, 2 * SIDE, SIDE), F32)
    tile, plane = (2, SIDE, SIDE), (SIDE, SIDE)
    given = [own, right, below, diag]
    in_splits = [len(x) > 1 for x in given]
    shapes = [jax.ShapeDtypeStruct(s, F32) for x in out_splits for s in ([plane] * 2 if x else [tile])]
    sums = iter(
        pl.pallas_call(
            functools.partial(update_kernel, in_splits, out_splits),
            out_shape=shapes,
            in_specs=[SMEM, SMEM] + [VMEM] * (sum(map(len, given)) + 3),
            out_specs=[VMEM] * len(shapes),
            scratch_shapes=[
                tall,
                tall,
                tall,
                tall,
                pltpu.VMEM(tile, F32),
                pltpu.VMEM((modes, 2, SIDE, SIDE), F32),
                pltpu.VMEM((modes, 2, SIDE, SIDE), BF16),
                pltpu.VMEM(tile, F32),
            ],
            compiler_params=pltpu.CompilerParams(vmem_limit_bytes=24 * 2**20),
        )(offsets, count, *own, *right, *below, *diag, probe, amplitude, table)
    )
    return [[next(sums) for _ in range(2 if x else 1)] for x in out_splits]


def body(object_field, probe_modes, positions, counts, amplitude):
    table = tables()
    sorted_amp = sort_amplitude(amplitude[0, 0])
    def planes(arrays):
        return arrays if len(arrays) > 1 else [arrays[0][part] for part in (0, 1)]

    def shaped(arrays, split):
        if split:
            return planes(arrays)
        return arrays if len(arrays) == 1 else [jnp.stack(arrays)]

    field = [object_field]
    for sweep in range(ITERS):
        h_split = H_SPLIT[sweep]
        g_split = G_SPLIT[sweep]
        right = [from_behind(f, "col", -1) for f in shaped(field, h_split[1])]
        below = [from_behind(f, "row", -1) for f in shaped(field, h_split[2])]
        diag = [from_behind(b, "col", -1) for b in below]
        own_sum, right_sum, below_sum, diag_sum = gradient(
            positions, counts, field, right, below, diag, probe_modes, sorted_amp, table, g_split
        )
        diag_sum = [from_behind(d, "col", 1) for d in diag_sum]
        from_above = [from_behind(b + d, "row", 1) for b, d in zip(below_sum, diag_sum)]
        from_left = [from_behind(r, "col", 1) for r in right_sum]
        if g_split[2]:
            field = [
                lax.optimization_barrier(f - STEP * (o + l + a))
                for f, o, l, a in zip(planes(field), planes(own_sum), planes(from_left), from_above)
            ]
        else:
            field = [field[0] - STEP * (own_sum[0] + from_left[0] + from_above[0])]
    return shaped(field, False)[0]


def solution(mesh):
    placed = (
        P(None, "row", "col"),
        P(),
        P("row", "col", None, None),
        P("row", "col"),
        P("row", "col", None, None, None),
    )
    return jax.shard_map(
        body, mesh=mesh, in_specs=placed, out_specs=P(None, "row", "col"), check_vma=False
    )
```

```python
import functools
import math

import jax
import jax.numpy as jnp
import ml_dtypes
import numpy as np
from jax import lax
from jax.experimental import pallas as pl
from jax.experimental.pallas import tpu as pltpu
from jax.sharding import PartitionSpec as P

ITERS = 2
STEP = 0.1
DAMPING = 0.1
SIDE = 256
HALF = 128
SUB = 8
CHUNK = 16
H_SPLIT = [[False, False, True, True], [True, False, True, True]]
G_SPLIT = [[True, False, True, True], [True, False, True, True]]
AHEAD = 1
F32 = jnp.float32
BF16 = jnp.bfloat16
VMEM = pl.BlockSpec(memory_space=pltpu.VMEM)
SMEM = pl.BlockSpec(memory_space=pltpu.SMEM)


def from_behind(block, axis, distance):
    size = lax.axis_size(axis)
    return lax.ppermute(block, axis, [(i, (i + distance) % size) for i in range(size)])


def tables():
    ladder = np.arange(SIDE, dtype=np.int32)
    theta = (ladder[:, None] * ladder[None, :] % SIDE).astype(np.float32)
    theta = theta * np.float32(2.0 * math.pi / SIDE)
    factor = np.float32(1.0 / math.sqrt(SIDE))
    cosine, sine = np.cos(theta) * factor, np.sin(theta) * factor
    forms = []
    for parity in (0, 1):
        c, s = cosine[parity::2, :HALF], sine[parity::2, :HALF]
        forms.append(np.block([[c, s], [-s, c]]))
    forms += [f.T for f in forms]
    return np.stack(forms).astype(ml_dtypes.bfloat16)


def parity_order():
    order = np.concatenate([np.arange(0, SIDE, 2), np.arange(1, SIDE, 2)])
    matrix = np.zeros((SIDE, SIDE), np.float32)
    matrix[order, np.arange(SIDE)] = 1.0
    return matrix.astype(ml_dtypes.bfloat16)


def sort_kernel(order_ref, amp_ref, out_ref, wide):
    def one(slot, _):
        rest, terms = amp_ref[slot], []
        for _ in range(3):
            terms.append(rest.astype(BF16))
            rest = rest - terms[-1].astype(F32)
        moved = [dot(term, order_ref[...]) for term in terms]
        whole = (moved[0] + moved[1]) + moved[2]
        for q in (0, 1):
            at = slice(q * HALF, (q + 1) * HALF)
            wide[q] = whole[:, at]
            for parity in (0, 1):
                rows_at = pl.ds(parity * HALF, HALF)
                out_ref[slot, rows_at, at] = wide[q, pl.ds(parity, HALF, stride=2), :]
        return 0

    lax.fori_loop(0, amp_ref.shape[0], one, 0)


def sort_amplitude(amplitude):
    return pl.pallas_call(
        sort_kernel,
        out_shape=jax.ShapeDtypeStruct(amplitude.shape, F32),
        in_specs=[VMEM, VMEM],
        out_specs=VMEM,
        scratch_shapes=[pltpu.VMEM((2, SIDE, HALF), F32)],
        compiler_params=pltpu.CompilerParams(vmem_limit_bytes=16 * 2**20),
        cost_estimate=pl.CostEstimate(
            flops=6 * amplitude.size * SIDE, bytes_accessed=8 * amplitude.size, transcendentals=0
        ),
    )(parity_order(), amplitude)


def dot(a, b):
    return jnp.dot(a, b, preferred_element_type=F32)


def lanes(a, b):
    return jnp.concatenate([a, b], axis=1)


def rows(a, b):
    return jnp.concatenate([a, b], axis=0)


def in_turn(modes, first, second):
    held = []
    for m in range(modes + AHEAD):
        if m < modes:
            held.append(first(m))
        if m >= AHEAD:
            second(m - AHEAD, held[m - AHEAD])


def places(splits):
    found = []
    for index, split in enumerate(splits):
        at = pl.ds(index // 2 * SIDE, SIDE)
        for part in (0, 1) if split else (slice(None),):
            found.append((index % 2, part, at))
    return found


def update_kernel(in_splits, out_splits, offsets_ref, count_ref, *refs):
    tile_at, out_at = places(in_splits), places(out_splits)
    tiles, refs = refs[: len(tile_at)], refs[len(tile_at) :]
    (probe_ref, amp_ref, table_ref), refs = refs[:3], refs[3:]
    outs, scratch = refs[: len(out_at)], refs[len(out_at) :]
    left_ext, right_ext, left_sum, right_sum, patch, far, chis, grad = scratch
    modes = probe_ref.shape[0]
    row_inside = lax.axis_index("row") < lax.axis_size("row") - 1
    col_inside = lax.axis_index("col") < lax.axis_size("col") - 1

    def masked(values, half, at):
        if half:
            values = jnp.where(col_inside, values, 0.0)
        return jnp.where(row_inside, values, 0.0) if at.start else values

    for tile, (half, part, at) in zip(tiles, tile_at):
        (left_ext, right_ext)[half][part, at] = masked(tile[...], half, at)
    left_sum[...] = jnp.zeros_like(left_sum)
    right_sum[...] = jnp.zeros_like(right_sum)
    groups = SIDE // SUB
    column = lax.broadcasted_iota(jnp.int32, (SIDE + SUB, SIDE), 1)
    lane = lax.broadcasted_iota(jnp.int32, (groups, SUB, SIDE), 1)

    def position(slot, _):
        top, left = offsets_ref[0, 0, slot, 0], offsets_ref[0, 0, slot, 1]
        shift = lax.rem(top, SUB)
        window = pl.ds(pl.multiple_of(top - shift, SUB), SIDE + SUB)
        beside = column >= left
        for part in (0, 1):
            mixed = jnp.where(beside, left_ext[part, window, :], right_ext[part, window, :])
            mixed = pltpu.roll(mixed, lax.rem(SIDE - left, SIDE), 1)
            mixed = mixed.reshape(groups + 1, SUB, SIDE)
            mixed = pltpu.roll(mixed, lax.rem(SUB - shift, SUB), 1)
            mixed = jnp.where(lane < SUB - shift, mixed[:-1], mixed[1:])
            patch[part] = mixed.reshape(SIDE, SIDE)
        def section(m):
            psi = []
            for half in (0, 1):
                at = pl.ds(half * HALF, HALF)
                pr, pi = probe_ref[m, 0, at, :], probe_ref[m, 1, at, :]
                xr, xi = patch[0, at, :], patch[1, at, :]
                psi.append(rows(pr * xr - pi * xi, pr * xi + pi * xr))
            even = dot(table_ref[0], (psi[0] + psi[1]).astype(BF16))
            odd = dot(table_ref[1], (psi[0] - psi[1]).astype(BF16))
            sums, differences = [], []
            for s in (even, odd):
                a, b = s[:, :HALF], s[:, HALF:]
                u, v = (a + b).astype(BF16), (a - b).astype(BF16)
                sums.append(lanes(u[:HALF], u[HALF:]))
                differences.append(lanes(v[:HALF], v[HALF:]))
            return rows(*sums), rows(*differences)

        def spread(m, blocks):
            for q, block in enumerate(blocks):
                far[m, q] = dot(block, table_ref[2 + q])

        def back(m):
            halves = []
            for parity in (0, 1):
                at = pl.ds(parity * HALF, HALF)
                c = [chis[m, q, at, :] for q in (0, 1)]
                real = lanes(c[0][:, :HALF], c[1][:, :HALF])
                imag = lanes(c[0][:, HALF:], c[1][:, HALF:])
                halves.append(dot(table_ref[2 + parity], rows(real, imag)))
            top_back = (halves[0] + halves[1]).astype(BF16)
            bottom_back = (halves[0] - halves[1]).astype(BF16)
            blocks = []
            for q in (0, 1):
                at = slice(q * HALF, (q + 1) * HALF)
                blocks.append(
                    rows(
                        lanes(top_back[:HALF, at], top_back[HALF:, at]),
                        lanes(bottom_back[:HALF, at], bottom_back[HALF:, at]),
                    )
                )
            return blocks

        def gather(m, blocks):
            wave = [dot(block, table_ref[q]) for q, block in enumerate(blocks)]
            for side, w in ((0, wave[0] + wave[1]), (1, wave[0] - wave[1])):
                at = pl.ds(side * HALF, HALF)
                pr, pi = probe_ref[m, 0, :, at], probe_ref[m, 1, :, at]
                wr, wi = w[:, :HALF], w[:, HALF:]
                gr, gi = pr * wr + pi * wi, pr * wi - pi * wr
                if m:
                    gr, gi = gr + grad[0, :, at], gi + grad[1, :, at]
                grad[0, :, at] = gr
                grad[1, :, at] = gi

        in_turn(modes, section, spread)
        for q in (0, 1):
            for start in range(0, SIDE, CHUNK):
                at = pl.ds(start, CHUNK)
                f = [far[m, q, at, :] for m in range(modes)]
                squares = [x * x for x in f]
                power = sum(squares[1:], squares[0])
                power = power[:, :HALF] + power[:, HALF:]
                measured = amp_ref[slot, at, q * HALF : (q + 1) * HALF]
                ratio = 1.0 - measured * lax.rsqrt(power + DAMPING)
                ratio = lanes(ratio, ratio)
                for m in range(modes):
                    chis[m, q, at, :] = (f[m] * ratio).astype(BF16)
        in_turn(modes, back, gather)
        empty = jnp.zeros((1, SUB, SIDE), F32)
        for part in (0, 1):
            turned = pltpu.roll(grad[part], left, 1).reshape(groups, SUB, SIDE)
            turned = pltpu.roll(turned, shift, 1)
            first = jnp.concatenate([jnp.where(lane < shift, 0.0, turned), empty], axis=0)
            second = jnp.concatenate([empty, jnp.where(lane < shift, turned, 0.0)], axis=0)
            turned = (first + second).reshape(SIDE + SUB, SIDE)
            left_sum[part, window, :] += jnp.where(beside, turned, 0.0)
            right_sum[part, window, :] += jnp.where(beside, 0.0, turned)
        return 0

    lax.fori_loop(0, count_ref[0, 0], position, 0)
    for out, (half, part, at) in zip(outs, out_at):
        out[...] = masked((left_sum, right_sum)[half][part, at], half, at)


def gradient(offsets, count, own, right, below, diag, probe, amplitude, table, out_splits):
    modes = probe.shape[0]
    tall = pltpu.VMEM((2, 2 * SIDE, SIDE), F32)
    tile, plane = (2, SIDE, SIDE), (SIDE, SIDE)
    given = [own, right, below, diag]
    in_splits = [len(x) > 1 for x in given]
    shapes = [jax.ShapeDtypeStruct(s, F32) for x in out_splits for s in ([plane] * 2 if x else [tile])]
    sums = iter(
        pl.pallas_call(
            functools.partial(update_kernel, in_splits, out_splits),
            out_shape=shapes,
            in_specs=[SMEM, SMEM] + [VMEM] * (sum(map(len, given)) + 3),
            out_specs=[VMEM] * len(shapes),
            scratch_shapes=[
                tall,
                tall,
                tall,
                tall,
                pltpu.VMEM(tile, F32),
                pltpu.VMEM((modes, 2, SIDE, SIDE), F32),
                pltpu.VMEM((modes, 2, SIDE, SIDE), BF16),
                pltpu.VMEM(tile, F32),
            ],
            compiler_params=pltpu.CompilerParams(vmem_limit_bytes=24 * 2**20),
        )(offsets, count, *own, *right, *below, *diag, probe, amplitude, table)
    )
    return [[next(sums) for _ in range(2 if x else 1)] for x in out_splits]


def body(object_field, probe_modes, positions, counts, amplitude):
    table = tables()
    sorted_amp = sort_amplitude(amplitude[0, 0])
    def planes(arrays):
        return arrays if len(arrays) > 1 else [arrays[0][part] for part in (0, 1)]

    def shaped(arrays, split):
        if split:
            return planes(arrays)
        return arrays if len(arrays) == 1 else [jnp.stack(arrays)]

    field = [object_field]
    for sweep in range(ITERS):
        h_split = H_SPLIT[sweep]
        g_split = G_SPLIT[sweep]
        right = [from_behind(f, "col", -1) for f in shaped(field, h_split[1])]
        below = [from_behind(f, "row", -1) for f in shaped(field, h_split[2])]
        diag = [from_behind(b, "col", -1) for b in below]
        own_sum, right_sum, below_sum, diag_sum = gradient(
            positions, counts, field, right, below, diag, probe_modes, sorted_amp, table, g_split
        )
        diag_sum = [from_behind(d, "col", 1) for d in diag_sum]
        from_above = [from_behind(b + d, "row", 1) for b, d in zip(below_sum, diag_sum)]
        from_left = [from_behind(r, "col", 1) for r in right_sum]
        if g_split[2]:
            field = [
                lax.optimization_barrier(f - STEP * (o + l + a))
                for f, o, l, a in zip(planes(field), planes(own_sum), planes(from_left), from_above)
            ]
        else:
            field = [field[0] - STEP * (own_sum[0] + from_left[0] + from_above[0])]
    return shaped(field, False)[0]


def solution(mesh):
    placed = (
        P(None, "row", "col"),
        P(),
        P("row", "col", None, None),
        P("row", "col"),
        P("row", "col", None, None, None),
    )
    return jax.shard_map(
        body, mesh=mesh, in_specs=placed, out_specs=P(None, "row", "col"), check_vma=False
    )
```

```python
import functools
import math

import jax
import jax.numpy as jnp
import ml_dtypes
import numpy as np
from jax import lax
from jax.experimental import pallas as pl
from jax.experimental.pallas import tpu as pltpu
from jax.sharding import PartitionSpec as P

ITERS = 2
STEP = 0.1
DAMPING = 0.1
SIDE = 256
HALF = 128
SUB = 8
CHUNK = 16
CROSSED = (("col", -1), ("col", 1), ("row", -1))
H_SPLIT = [[False, True, True, True], [True, True, True, True]]
G_SPLIT = [[True, True, True, True], [True, True, True, True]]
AHEAD = 1
F32 = jnp.float32
BF16 = jnp.bfloat16
VMEM = pl.BlockSpec(memory_space=pltpu.VMEM)
SMEM = pl.BlockSpec(memory_space=pltpu.SMEM)


def from_behind(block, axis, distance):
    sizes = {"row": lax.axis_size("row"), "col": lax.axis_size("col")}
    route = []
    for r in range(sizes["row"]):
        for c in range(sizes["col"]):
            to = {"row": r, "col": c}
            to[axis] += distance
            if not 0 <= to[axis] < sizes[axis]:
                to[axis] %= sizes[axis]
                other = "col" if axis == "row" else "row"
                if (axis, distance) in CROSSED:
                    to[other] = (to[other] + sizes[other] // 2) % sizes[other]
            route.append((r * sizes["col"] + c, to["row"] * sizes["col"] + to["col"]))
    return lax.ppermute(block, ("row", "col"), route)


def tables():
    ladder = np.arange(SIDE, dtype=np.int32)
    theta = (ladder[:, None] * ladder[None, :] % SIDE).astype(np.float32)
    theta = theta * np.float32(2.0 * math.pi / SIDE)
    factor = np.float32(1.0 / math.sqrt(SIDE))
    cosine, sine = np.cos(theta) * factor, np.sin(theta) * factor
    forms = []
    for parity in (0, 1):
        c, s = cosine[parity::2, :HALF], sine[parity::2, :HALF]
        forms.append(np.block([[c, s], [-s, c]]))
    forms += [f.T for f in forms]
    return np.stack(forms).astype(ml_dtypes.bfloat16)


def parity_order():
    order = np.concatenate([np.arange(0, SIDE, 2), np.arange(1, SIDE, 2)])
    matrix = np.zeros((SIDE, SIDE), np.float32)
    matrix[order, np.arange(SIDE)] = 1.0
    return matrix.astype(ml_dtypes.bfloat16)


def sort_kernel(order_ref, amp_ref, out_ref, wide):
    def one(slot, _):
        rest, terms = amp_ref[slot], []
        for _ in range(3):
            terms.append(rest.astype(BF16))
            rest = rest - terms[-1].astype(F32)
        moved = [dot(term, order_ref[...]) for term in terms]
        whole = (moved[0] + moved[1]) + moved[2]
        for q in (0, 1):
            at = slice(q * HALF, (q + 1) * HALF)
            wide[q] = whole[:, at]
            for parity in (0, 1):
                rows_at = pl.ds(parity * HALF, HALF)
                out_ref[slot, rows_at, at] = wide[q, pl.ds(parity, HALF, stride=2), :]
        return 0

    lax.fori_loop(0, amp_ref.shape[0], one, 0)


def sort_amplitude(amplitude):
    return pl.pallas_call(
        sort_kernel,
        out_shape=jax.ShapeDtypeStruct(amplitude.shape, F32),
        in_specs=[VMEM, VMEM],
        out_specs=VMEM,
        scratch_shapes=[pltpu.VMEM((2, SIDE, HALF), F32)],
        compiler_params=pltpu.CompilerParams(vmem_limit_bytes=16 * 2**20),
        cost_estimate=pl.CostEstimate(
            flops=6 * amplitude.size * SIDE, bytes_accessed=8 * amplitude.size, transcendentals=0
        ),
    )(parity_order(), amplitude)


def dot(a, b):
    return jnp.dot(a, b, preferred_element_type=F32)


def lanes(a, b):
    return jnp.concatenate([a, b], axis=1)


def rows(a, b):
    return jnp.concatenate([a, b], axis=0)


def in_turn(modes, first, second):
    held = []
    for m in range(modes + AHEAD):
        if m < modes:
            held.append(first(m))
        if m >= AHEAD:
            second(m - AHEAD, held[m - AHEAD])


def places(splits):
    found = []
    for index, split in enumerate(splits):
        at = pl.ds(index // 2 * SIDE, SIDE)
        for part in (0, 1) if split else (slice(None),):
            found.append((index % 2, part, at))
    return found


def update_kernel(in_splits, out_splits, offsets_ref, count_ref, *refs):
    tile_at, out_at = places(in_splits), places(out_splits)
    tiles, refs = refs[: len(tile_at)], refs[len(tile_at) :]
    (probe_ref, amp_ref, table_ref), refs = refs[:3], refs[3:]
    outs, scratch = refs[: len(out_at)], refs[len(out_at) :]
    left_ext, right_ext, left_sum, right_sum, patch, far, chis, grad = scratch
    modes = probe_ref.shape[0]
    row_inside = lax.axis_index("row") < lax.axis_size("row") - 1
    col_inside = lax.axis_index("col") < lax.axis_size("col") - 1

    def masked(values, half, at):
        if half:
            values = jnp.where(col_inside, values, 0.0)
        return jnp.where(row_inside, values, 0.0) if at.start else values

    for tile, (half, part, at) in zip(tiles, tile_at):
        (left_ext, right_ext)[half][part, at] = masked(tile[...], half, at)
    left_sum[...] = jnp.zeros_like(left_sum)
    right_sum[...] = jnp.zeros_like(right_sum)
    groups = SIDE // SUB
    column = lax.broadcasted_iota(jnp.int32, (SIDE + SUB, SIDE), 1)
    lane = lax.broadcasted_iota(jnp.int32, (groups, SUB, SIDE), 1)

    def position(slot, _):
        top, left = offsets_ref[0, 0, slot, 0], offsets_ref[0, 0, slot, 1]
        shift = lax.rem(top, SUB)
        window = pl.ds(pl.multiple_of(top - shift, SUB), SIDE + SUB)
        beside = column >= left
        for part in (0, 1):
            mixed = jnp.where(beside, left_ext[part, window, :], right_ext[part, window, :])
            mixed = pltpu.roll(mixed, lax.rem(SIDE - left, SIDE), 1)
            mixed = mixed.reshape(groups + 1, SUB, SIDE)
            mixed = pltpu.roll(mixed, lax.rem(SUB - shift, SUB), 1)
            mixed = jnp.where(lane < SUB - shift, mixed[:-1], mixed[1:])
            patch[part] = mixed.reshape(SIDE, SIDE)
        def section(m):
            psi = []
            for half in (0, 1):
                at = pl.ds(half * HALF, HALF)
                pr, pi = probe_ref[m, 0, at, :], probe_ref[m, 1, at, :]
                xr, xi = patch[0, at, :], patch[1, at, :]
                psi.append(rows(pr * xr - pi * xi, pr * xi + pi * xr))
            even = dot(table_ref[0], (psi[0] + psi[1]).astype(BF16))
            odd = dot(table_ref[1], (psi[0] - psi[1]).astype(BF16))
            sums, differences = [], []
            for s in (even, odd):
                a, b = s[:, :HALF], s[:, HALF:]
                u, v = (a + b).astype(BF16), (a - b).astype(BF16)
                sums.append(lanes(u[:HALF], u[HALF:]))
                differences.append(lanes(v[:HALF], v[HALF:]))
            return rows(*sums), rows(*differences)

        def spread(m, blocks):
            for q, block in enumerate(blocks):
                far[m, q] = dot(block, table_ref[2 + q])

        def back(m):
            halves = []
            for parity in (0, 1):
                at = pl.ds(parity * HALF, HALF)
                c = [chis[m, q, at, :] for q in (0, 1)]
                real = lanes(c[0][:, :HALF], c[1][:, :HALF])
                imag = lanes(c[0][:, HALF:], c[1][:, HALF:])
                halves.append(dot(table_ref[2 + parity], rows(real, imag)))
            top_back = (halves[0] + halves[1]).astype(BF16)
            bottom_back = (halves[0] - halves[1]).astype(BF16)
            blocks = []
            for q in (0, 1):
                at = slice(q * HALF, (q + 1) * HALF)
                blocks.append(
                    rows(
                        lanes(top_back[:HALF, at], top_back[HALF:, at]),
                        lanes(bottom_back[:HALF, at], bottom_back[HALF:, at]),
                    )
                )
            return blocks

        def gather(m, blocks):
            wave = [dot(block, table_ref[q]) for q, block in enumerate(blocks)]
            for side, w in ((0, wave[0] + wave[1]), (1, wave[0] - wave[1])):
                at = pl.ds(side * HALF, HALF)
                pr, pi = probe_ref[m, 0, :, at], probe_ref[m, 1, :, at]
                wr, wi = w[:, :HALF], w[:, HALF:]
                gr, gi = pr * wr + pi * wi, pr * wi - pi * wr
                if m:
                    gr, gi = gr + grad[0, :, at], gi + grad[1, :, at]
                grad[0, :, at] = gr
                grad[1, :, at] = gi

        in_turn(modes, section, spread)
        for q in (0, 1):
            for start in range(0, SIDE, CHUNK):
                at = pl.ds(start, CHUNK)
                f = [far[m, q, at, :] for m in range(modes)]
                squares = [x * x for x in f]
                power = sum(squares[1:], squares[0])
                power = power[:, :HALF] + power[:, HALF:]
                measured = amp_ref[slot, at, q * HALF : (q + 1) * HALF]
                ratio = 1.0 - measured * lax.rsqrt(power + DAMPING)
                ratio = lanes(ratio, ratio)
                for m in range(modes):
                    chis[m, q, at, :] = (f[m] * ratio).astype(BF16)
        in_turn(modes, back, gather)
        empty = jnp.zeros((1, SUB, SIDE), F32)
        for part in (0, 1):
            turned = pltpu.roll(grad[part], left, 1).reshape(groups, SUB, SIDE)
            turned = pltpu.roll(turned, shift, 1)
            first = jnp.concatenate([jnp.where(lane < shift, 0.0, turned), empty], axis=0)
            second = jnp.concatenate([empty, jnp.where(lane < shift, turned, 0.0)], axis=0)
            turned = (first + second).reshape(SIDE + SUB, SIDE)
            left_sum[part, window, :] += jnp.where(beside, turned, 0.0)
            right_sum[part, window, :] += jnp.where(beside, 0.0, turned)
        return 0

    lax.fori_loop(0, count_ref[0, 0], position, 0)
    for out, (half, part, at) in zip(outs, out_at):
        out[...] = masked((left_sum, right_sum)[half][part, at], half, at)


def gradient(offsets, count, own, right, below, diag, probe, amplitude, table, out_splits):
    modes = probe.shape[0]
    tall = pltpu.VMEM((2, 2 * SIDE, SIDE), F32)
    tile, plane = (2, SIDE, SIDE), (SIDE, SIDE)
    given = [own, right, below, diag]
    in_splits = [len(x) > 1 for x in given]
    shapes = [jax.ShapeDtypeStruct(s, F32) for x in out_splits for s in ([plane] * 2 if x else [tile])]
    sums = iter(
        pl.pallas_call(
            functools.partial(update_kernel, in_splits, out_splits),
            out_shape=shapes,
            in_specs=[SMEM, SMEM] + [VMEM] * (sum(map(len, given)) + 3),
            out_specs=[VMEM] * len(shapes),
            scratch_shapes=[
                tall,
                tall,
                tall,
                tall,
                pltpu.VMEM(tile, F32),
                pltpu.VMEM((modes, 2, SIDE, SIDE), F32),
                pltpu.VMEM((modes, 2, SIDE, SIDE), BF16),
                pltpu.VMEM(tile, F32),
            ],
            compiler_params=pltpu.CompilerParams(vmem_limit_bytes=24 * 2**20),
        )(offsets, count, *own, *right, *below, *diag, probe, amplitude, table)
    )
    return [[next(sums) for _ in range(2 if x else 1)] for x in out_splits]


def body(object_field, probe_modes, positions, counts, amplitude):
    table = tables()
    sorted_amp = sort_amplitude(amplitude[0, 0])
    def planes(arrays):
        return arrays if len(arrays) > 1 else [arrays[0][part] for part in (0, 1)]

    def shaped(arrays, split):
        if split:
            return planes(arrays)
        return arrays if len(arrays) == 1 else [jnp.stack(arrays)]

    field = [object_field]
    for sweep in range(ITERS):
        h_split = H_SPLIT[sweep]
        g_split = G_SPLIT[sweep]
        right = [from_behind(f, "col", -1) for f in shaped(field, h_split[1])]
        below = [from_behind(f, "row", -1) for f in shaped(field, h_split[2])]
        diag = [from_behind(b, "col", -1) for b in below]
        own_sum, right_sum, below_sum, diag_sum = gradient(
            positions, counts, field, right, below, diag, probe_modes, sorted_amp, table, g_split
        )
        diag_sum = [from_behind(d, "col", 1) for d in diag_sum]
        from_above = [from_behind(b + d, "row", 1) for b, d in zip(below_sum, diag_sum)]
        from_left = [from_behind(r, "col", 1) for r in right_sum]
        if g_split[2]:
            field = [
                lax.optimization_barrier(f - STEP * (o + l + a))
                for f, o, l, a in zip(planes(field), planes(own_sum), planes(from_left), from_above)
            ]
        else:
            field = [field[0] - STEP * (own_sum[0] + from_left[0] + from_above[0])]
    return shaped(field, False)[0]


def solution(mesh):
    placed = (
        P(None, "row", "col"),
        P(),
        P("row", "col", None, None),
        P("row", "col"),
        P("row", "col", None, None, None),
    )
    return jax.shard_map(
        body, mesh=mesh, in_specs=placed, out_specs=P(None, "row", "col"), check_vma=False
    )
```
